128 devices in a mesh: section: 2 (over y_hi), ep: 16 (over y_lo, z, core), edp: 4 (over x).
Axes of the slice: x: 4, y: 4 (y_hi: 2, y_lo: 2; y = y_hi * 2 + y_lo), z: 4, core: 2. Of those that a mesh axis runs over, the one named last changes fastest.
Arguments:
- tokens: bfloat16 [2, 6144, 5120], P('section', 'ep', 'edp'), may hold values from -6 to 6
- out_grads: bfloat16 [2, 6144, 5120], P('section', 'ep', 'edp'), may hold values from -6 to 6
- gates: bfloat16 [2, 6144, 6], P('section', 'ep'), may hold values from 0.099609375 to 1.5
- routes: int32 [2, 6144, 6], P('section', 'ep'), may hold values from 0 to 159, as said below
- w_gate: bfloat16 [2, 16, 5120, 1536], P('section', 'ep', None, 'edp'), may hold values from -0.078125 to 0.078125
- w_up: bfloat16 [2, 16, 5120, 1536], P('section', 'ep', None, 'edp'), may hold values from -0.078125 to 0.078125
- w_down: bfloat16 [2, 16, 1536, 5120], P('section', 'ep', 'edp'), may hold values from -0.15625 to 0.15625
Outputs:
- grad_prev: bfloat16 [2, 6144, 5120], P('section', 'ep', 'edp')
- grad_w_gate: bfloat16 [2, 16, 5120, 1536], P('section', 'ep', None, 'edp')
- grad_w_up: bfloat16 [2, 16, 5120, 1536], P('section', 'ep', None, 'edp')
- grad_w_down: bfloat16 [2, 16, 1536, 5120], P('section', 'ep', 'edp')
The draws below stay inside these ranges and needn't reach their ends.
Inputs may be any that keep to these rules, and one draw needn't show every extreme that they name: `routes`: each row names 6 different experts. Within one section, the rows of one index of ep name each window expert (an id that is a multiple of 10) at most 24 times; in every section some window expert is named exactly 24 times by the rows of every index of ep.
All inputs are finite; a program needn't handle non-finite values.
Results may differ from the reference program's by a relative error of at most 0.013.
Values may be sent and summed in bfloat16 or wider, within the bound.
No kernel may reach another device: no remote copies, remote signals or barrier semaphores. Data moves between devices by JAX's collectives and lax.ppermute only.
A program may use at most 128 MiB of HBM per device.

```python
import math
from functools import partial
import jax
import jax.numpy as jnp
from jax import lax

D = 5120
FF = 1536
EXPERTS = 160
TOP = 6
TOK_EP = 384
CAP = 24
TOKENS = 6144
N_SECTION = 2
N_EP = 16
N_EDP = 4


def draw_routes(key, part):
    key = jax.random.fold_in(key, 7)
    group_size = EXPERTS // N_EP
    key_list = jax.random.split(key, 7)
    popular = jax.random.randint(key_list[0], (N_SECTION, 1, N_EP), 1, 5)
    jitter = jax.random.randint(key_list[1], (N_SECTION, N_EP, N_EP), 8, 17)
    counts = jnp.minimum(CAP, CAP * popular * jitter // 64)
    window = jnp.arange(N_EP, dtype=jnp.int32)
    full_section = jax.random.randint(key_list[2], (N_SECTION, 1, 1), 0, N_EP)
    full_block = jax.random.randint(key_list[3], (N_SECTION, N_EP, 1), 0, N_EP)
    counts = jnp.where((window == full_section) | (window == full_block), CAP, counts)
    bounds = jnp.cumsum(counts, axis=-1)
    places = jnp.arange(TOK_EP * TOP, dtype=jnp.int32)
    owners = jnp.sum((places[None, None, :, None] >= bounds[:, :, None, :]).astype(jnp.int32), axis=-1)
    owners = jnp.swapaxes(owners.reshape(N_SECTION, N_EP, TOP, TOK_EP), 2, 3)
    inside = owners < N_EP
    others = EXPERTS - N_EP
    scores = jax.random.randint(key_list[4], (N_SECTION, N_EP, TOK_EP, others), 0, 1 << 16) * others + jnp.arange(others, dtype=jnp.int32)
    picked = lax.top_k(scores, TOP)[1]
    other_ids = picked // (group_size - 1) * group_size + 1 + picked % (group_size - 1)
    chosen = jnp.where(inside, owners * group_size, other_ids)
    row_scores = jax.random.randint(key_list[5], (N_SECTION, N_EP, TOK_EP), 0, 1 << 16) * TOK_EP + jnp.arange(TOK_EP, dtype=jnp.int32)
    row_order = jnp.argsort(row_scores, axis=-1)
    chosen = jnp.take_along_axis(chosen, row_order[..., None], axis=2)
    route_scores = jax.random.randint(key_list[6], (N_SECTION, N_EP, TOK_EP, TOP), 0, 1 << 16) * TOP + jnp.arange(TOP, dtype=jnp.int32)
    route_order = jnp.argsort(route_scores, axis=-1)
    chosen = jnp.take_along_axis(chosen, route_order, axis=3)
    return chosen.reshape(N_SECTION, N_EP * TOK_EP, TOP).astype(jnp.int32)


def shard_levels(stream_key, dims, cuts, low, largest):
    level = 1.0
    for axis_at, parts in cuts:
        steps = jax.random.uniform(jax.random.fold_in(jax.random.fold_in(stream_key, 6), axis_at), (parts,), jnp.float32, low / len(cuts), largest / len(cuts))
        level = level * jnp.repeat(jnp.exp(steps), dims[axis_at] // parts).reshape((-1,) + (1,) * (len(dims) - 1 - axis_at))
    return level


def scatter_about(stream_key, dims, width, most, pieces=(), kind=jnp.bfloat16):
    loudness = shard_levels(stream_key, dims, pieces, -0.22, 0.18) if pieces else 1.0
    result = jax.random.normal(stream_key, dims, jnp.float32) * width * loudness
    return jnp.minimum(jnp.maximum(result, -most), most).astype(kind)


def setup_inputs(seed: int = 0) -> dict:
    arg_keys = jax.random.split(jax.random.key(seed), 8)
    tokens = scatter_about(arg_keys[0], (N_SECTION, TOKENS, D), 1.0, 6.0, ((0, 2), (1, 16), (2, 4)))
    out_grads = scatter_about(arg_keys[1], (N_SECTION, TOKENS, D), 1.0, 6.0, ((0, 2), (1, 16), (2, 4)))
    gates = jnp.clip(jnp.exp(math.log(1.5) - 2.7119641 * jax.random.uniform(arg_keys[2], (N_SECTION, TOKENS, TOP), jnp.float32) ** shard_levels(arg_keys[2], (N_SECTION, TOKENS, TOP), ((0, 2), (1, 16)), -0.2, 0.2)), 0.099609375, 1.5).astype(jnp.bfloat16)
    routes = draw_routes(jax.random.fold_in(arg_keys[7], 71), 0)
    w_gate = scatter_about(arg_keys[4], (N_SECTION, N_EP, D, FF), D ** -0.5, 0.078125, ((0, 2), (1, 16), (3, 4)))
    w_up = scatter_about(arg_keys[5], (N_SECTION, N_EP, D, FF), D ** -0.5, 0.078125, ((0, 2), (1, 16), (3, 4)))
    w_down = scatter_about(arg_keys[6], (N_SECTION, N_EP, FF, D), FF ** -0.5, 0.15625, ((0, 2), (1, 16), (2, 4)))
    return {"tokens": tokens, "out_grads": out_grads, "gates": gates, "routes": routes, "w_gate": w_gate, "w_up": w_up, "w_down": w_down}


def route_targets(block_routes):
    group_size = EXPERTS // N_EP
    flat_routes = block_routes.reshape(-1)
    inside = (flat_routes % group_size) == 0
    expert_slot = (flat_routes // group_size).astype(jnp.int32)
    matches = ((expert_slot[:, None] == jnp.arange(N_EP, dtype=jnp.int32)[None, :]) & inside[:, None]).astype(jnp.int32)
    earlier = jnp.cumsum(matches, axis=0).astype(jnp.int32) - matches
    position = jnp.sum(earlier * matches, axis=1).astype(jnp.int32)
    return jnp.where(inside, expert_slot * CAP + position, N_EP * CAP).astype(jnp.int32)


def slot_owners(targets):
    token_index = jnp.arange(TOK_EP * TOP, dtype=jnp.int32) // TOP
    empty_owner = jnp.full((N_EP * CAP,), TOK_EP, jnp.int32)
    return empty_owner.at[targets].set(token_index, mode="drop")


def slot_gates(block_gates, targets):
    empty_gate = jnp.zeros((N_EP * CAP,), block_gates.dtype)
    return empty_gate.at[targets].set(block_gates.reshape(-1), mode="drop")


def expert_grads(bundle):
    rows_x, rows_dy, row_gate, gate_weight, up_weight, down_weight = bundle
    gate_pre = jnp.dot(rows_x, gate_weight, preferred_element_type=jnp.float32)
    up_pre = jnp.dot(rows_x, up_weight, preferred_element_type=jnp.float32)
    back = jnp.dot(rows_dy, down_weight.T, preferred_element_type=jnp.float32)
    weight = row_gate.astype(jnp.float32)[:, None]
    sigmoid_gate = jax.nn.sigmoid(gate_pre)
    swish = gate_pre * sigmoid_gate
    hidden = swish * up_pre
    d_hidden = weight * back
    d_gate = (d_hidden * up_pre * sigmoid_gate * (1.0 + gate_pre * (1.0 - sigmoid_gate))).astype(jnp.bfloat16)
    d_up = (d_hidden * swish).astype(jnp.bfloat16)
    gated_hidden = (weight * hidden).astype(jnp.bfloat16)
    grad_gate = jnp.dot(rows_x.T, d_gate, preferred_element_type=jnp.float32).astype(jnp.bfloat16)
    grad_up = jnp.dot(rows_x.T, d_up, preferred_element_type=jnp.float32).astype(jnp.bfloat16)
    grad_down = jnp.dot(gated_hidden.T, rows_dy, preferred_element_type=jnp.float32).astype(jnp.bfloat16)
    share_width = FF // N_EDP
    total = jnp.zeros((rows_x.shape[0], D), jnp.float32)
    for group_index in range(N_EDP):
        columns = slice(group_index * share_width, (group_index + 1) * share_width)
        piece = jnp.dot(d_gate[:, columns], gate_weight[:, columns].T, preferred_element_type=jnp.float32)
        piece = piece + jnp.dot(d_up[:, columns], up_weight[:, columns].T, preferred_element_type=jnp.float32)
        rounded = lax.optimization_barrier(piece.astype(jnp.bfloat16))
        total = total + rounded.astype(jnp.float32)
    return total.astype(jnp.bfloat16), grad_gate, grad_up, grad_down


def combine_block(bundle):
    slot_rows, targets = bundle
    picked = jnp.take(slot_rows, targets, axis=0, mode="fill", fill_value=0)
    picked = picked.astype(jnp.float32).reshape(TOK_EP, TOP, D)
    return jnp.sum(picked, axis=1).astype(jnp.bfloat16)


def to_experts(blocks):
    shaped = blocks.reshape((N_EP, N_EP, CAP) + blocks.shape[2:])
    moved = jnp.swapaxes(shaped, 0, 1)
    return moved.reshape((N_EP, N_EP * CAP) + blocks.shape[2:])


def reference(tokens, out_grads, gates, routes, w_gate, w_up, w_down):
    section_inputs = []
    gate_grads = []
    up_grads = []
    down_grads = []
    take_rows = jax.vmap(partial(jnp.take, axis=0, mode="fill", fill_value=0))
    for section_index in range(N_SECTION):
        block_routes = routes[section_index].reshape(N_EP, TOK_EP, TOP)
        targets = jax.vmap(route_targets)(block_routes)
        owners = jax.vmap(slot_owners)(targets)
        block_x = tokens[section_index].reshape(N_EP, TOK_EP, D)
        block_dy = out_grads[section_index].reshape(N_EP, TOK_EP, D)
        block_gates = gates[section_index].reshape(N_EP, TOK_EP, TOP)
        rows_x = to_experts(take_rows(block_x, owners))
        rows_dy = to_experts(take_rows(block_dy, owners))
        row_gate = to_experts(jax.vmap(slot_gates)(block_gates, targets))
        row_grads, grad_gate, grad_up, grad_down = lax.map(expert_grads, (rows_x, rows_dy, row_gate, w_gate[section_index], w_up[section_index], w_down[section_index]))
        returned = to_experts(row_grads)
        inputs = lax.map(combine_block, (returned, targets))
        section_inputs.append(inputs.reshape(TOKENS, D))
        gate_grads.append(grad_gate)
        up_grads.append(grad_up)
        down_grads.append(grad_down)
    grad_prev = jnp.roll(jnp.stack(section_inputs), -1, axis=0)
    return grad_prev, jnp.stack(gate_grads), jnp.stack(up_grads), jnp.stack(down_grads)
```

```python
import jax
import jax.numpy as jnp
from jax import lax
from jax.experimental import pallas as pl
from jax.experimental.pallas import tpu as pltpu
from jax.sharding import PartitionSpec as P

EXPERTS = 160
TOP = 6
CAP = 24
HALVES = 2
MIB = 1 << 20


def passed_along(array, axis, by):
    length = lax.axis_size(axis)
    return lax.ppermute(array, axis, [(i, (i + by) % length) for i in range(length)])


def contract(left, right, left_dim, right_dim):
    return lax.dot_general(
        left,
        right,
        (((left_dim,), (right_dim,)), ((), ())),
        preferred_element_type=jnp.float32,
    )


def slot_choice(routes_ref, gates_ref, ep_count):
    token_count = routes_ref.shape[0]
    per_half = CAP // HALVES
    half_rows = ep_count * per_half
    shape = (token_count, HALVES * half_rows)
    slot = lax.broadcasted_iota(jnp.int32, (1, shape[1]), 1)
    half = slot // half_rows
    within = slot - half * half_rows
    expert = within // per_half
    place = within - expert * per_half + half * per_half
    wanted = expert * (EXPERTS // ep_count)
    named = jnp.zeros(shape, jnp.float32)
    gate = jnp.zeros(shape, jnp.float32)
    for k in range(TOP):
        hit = routes_ref[:, k : k + 1] == wanted
        named = jnp.where(hit, 1.0, named)
        if gates_ref is not None:
            gate = jnp.where(hit, gates_ref[:, k : k + 1].astype(jnp.float32), gate)
    before = lax.broadcasted_iota(jnp.int32, (token_count, token_count), 1) < (
        lax.broadcasted_iota(jnp.int32, (token_count, token_count), 0)
    )
    earlier = contract(
        jnp.where(before, 1.0, 0.0).astype(jnp.bfloat16), named.astype(jnp.bfloat16), 1, 0
    )
    chosen = (named > 0.0) & (earlier == place.astype(jnp.float32))
    one = jnp.where(chosen, 1.0, 0.0).astype(jnp.bfloat16)
    if gates_ref is None:
        return one, None
    return one, jnp.where(chosen, gate, 0.0).astype(jnp.bfloat16)


def send_kernel(ep_count, routes_ref, gates_ref, x_ref, dy_ref, xa_ref, xb_ref, ya_ref, yb_ref):
    one, gate = slot_choice(routes_ref, gates_ref, ep_count)
    half_rows = one.shape[1] // HALVES
    for h, (x_out, y_out) in enumerate(((xa_ref, ya_ref), (xb_ref, yb_ref))):
        rows = slice(h * half_rows, (h + 1) * half_rows)
        x_out[...] = contract(one[:, rows], x_ref[...], 0, 0).astype(jnp.bfloat16)
        y_out[...] = contract(gate[:, rows], dy_ref[...], 0, 0).astype(jnp.bfloat16)


def choice_kernel(ep_count, routes_ref, a_ref, b_ref):
    one, _ = slot_choice(routes_ref, None, ep_count)
    half_rows = one.shape[1] // HALVES
    a_ref[...] = one[:, :half_rows]
    b_ref[...] = one[:, half_rows:]


def pre_kernel(me_ref, x0, x1, x2, x3, wg_ref, wu_ref, gate_ref, up_ref):
    step = pl.program_id(0)

    @pl.when(step == 0)
    def _():
        gate_ref[...] = jnp.zeros_like(gate_ref)
        up_ref[...] = jnp.zeros_like(up_ref)

    for d, x in enumerate((x0, x1, x2, x3)):

        @pl.when(step == d)
        def _(x=x):
            gate_ref[...] += contract(x[...], wg_ref[...], 1, 0)
            up_ref[...] += contract(x[...], wu_ref[...], 1, 0)


def mid_kernel(
    me_ref, y0, y1, y2, y3, gate_ref, up_ref, wd_ref, wg_ref, wu_ref,
    dg_ref, du_ref, gh_ref, p0, p1, p2, p3, back_ref,
):
    step = pl.program_id(0)

    @pl.when(step == 0)
    def _():
        back_ref[...] = jnp.zeros_like(back_ref)

    for d, y in enumerate((y0, y1, y2, y3)):

        @pl.when(step == d)
        def _(y=y):
            back_ref[...] += contract(y[...], wd_ref[...], 1, 1)

    @pl.when(step == 3)
    def _():
        gate_pre = gate_ref[...]
        up_pre = up_ref[...]
        d_hidden = back_ref[...]
        sigmoid = jax.nn.sigmoid(gate_pre)
        swish = gate_pre * sigmoid
        dg_ref[...] = (
            d_hidden * up_pre * sigmoid * (1.0 + gate_pre * (1.0 - sigmoid))
        ).astype(jnp.bfloat16)
        du_ref[...] = (d_hidden * swish).astype(jnp.bfloat16)
        gh_ref[...] = (swish * up_pre).astype(jnp.bfloat16)

    for d, p in enumerate((p0, p1, p2, p3)):

        @pl.when(step == 4 + d)
        def _(p=p):
            p[...] = (
                contract(dg_ref[...], wg_ref[...], 1, 1) + contract(du_ref[...], wu_ref[...], 1, 1)
            ).astype(jnp.bfloat16)


def grad_kernel(me_ref, *refs):
    xa, xb, ya, yb = refs[0:4], refs[4:8], refs[8:12], refs[12:16]
    dga, dgb, dua, dub, gha, ghb, out_g, out_u, out_d = refs[16:]
    step = pl.program_id(0)
    for d in range(4):

        @pl.when(step == d)
        def _(d=d):
            out_g[...] = (
                contract(xa[d][...], dga[...], 0, 0) + contract(xb[d][...], dgb[...], 0, 0)
            ).astype(jnp.bfloat16)
            out_u[...] = (
                contract(xa[d][...], dua[...], 0, 0) + contract(xb[d][...], dub[...], 0, 0)
            ).astype(jnp.bfloat16)
            out_d[...] = (
                contract(gha[...], ya[d][...], 0, 0) + contract(ghb[...], yb[d][...], 0, 0)
            ).astype(jnp.bfloat16)


def combine_kernel(ca_ref, cb_ref, a_ref, b_ref, out_ref):
    out_ref[...] = (
        contract(ca_ref[...], a_ref[...], 1, 0) + contract(cb_ref[...], b_ref[...], 1, 0)
    ).astype(jnp.bfloat16)


def bf16(*shape):
    return jax.ShapeDtypeStruct(shape, jnp.bfloat16)


def f32(*shape):
    return jax.ShapeDtypeStruct(shape, jnp.float32)


def whole(array):
    return pl.BlockSpec(array.shape, lambda *_: (0,) * len(array.shape))


def params(mib):
    return pltpu.CompilerParams(vmem_limit_bytes=mib * MIB)


ORDER = (0, 3, 1, 2)
SEND_ORDER = (2, 1, 3, 0)


def slice_at(order, step, me_ref):
    offset = jnp.int32(order[3])
    for d in range(3):
        offset = jnp.where(step == d, order[d], offset)
    return lax.rem(me_ref[0] + offset, 4)


def body(tokens, out_grads, gates, routes, w_gate, w_up, w_down):
    ep_count = lax.axis_size("ep")
    token_count, width = tokens.shape[1:]
    half_rows = ep_count * CAP // HALVES
    hidden = w_gate.shape[3]
    w_gate, w_up, w_down = w_gate[0, 0], w_up[0, 0], w_down[0, 0]
    me = lax.axis_index("edp").astype(jnp.int32).reshape(1)

    next_routes = passed_along(routes[0], "section", -1)

    sends = pl.pallas_call(
        lambda *refs: send_kernel(ep_count, *refs),
        out_shape=[bf16(half_rows, width)] * 4,
        compiler_params=params(32),
    )(routes[0], gates[0], tokens[0], out_grads[0])

    def to_experts(rows):
        shaped = rows.reshape(ep_count, CAP // HALVES, width)
        return lax.all_to_all(shaped, "ep", split_axis=0, concat_axis=0, tiled=True).reshape(
            half_rows, width
        )

    own = []
    for rows in (sends[0], sends[2], sends[1], sends[3]):
        own.append(to_experts(rows))
    own_x, own_y = (own[0], own[2]), (own[1], own[3])

    choice = pl.pallas_call(
        lambda *refs: choice_kernel(ep_count, *refs),
        out_shape=[bf16(token_count, half_rows)] * 2,
        compiler_params=params(16),
    )(next_routes)

    xs, ys, mids = [], [], []
    for h in range(HALVES):
        x_left = passed_along(own_x[h], "edp", 1)
        x_right = passed_along(own_x[h], "edp", -1)
        y_left = passed_along(own_y[h], "edp", 1)
        y_right = passed_along(own_y[h], "edp", -1)
        x_far = passed_along(x_left, "edp", 1)
        y_far = passed_along(y_right, "edp", -1)
        x = (own_x[h], x_left, x_right, x_far)
        y = (own_y[h], y_left, y_right, y_far)
        xs.append(x)
        ys.append(y)

        gate_pre, up_pre = pl.pallas_call(
            pre_kernel,
            out_shape=[f32(half_rows, hidden)] * 2,
            grid_spec=pltpu.PrefetchScalarGridSpec(
                num_scalar_prefetch=1,
                grid=(4,),
                in_specs=[whole(p) for p in x]
                + [
                    pl.BlockSpec((width, hidden), lambda i, m: (slice_at(ORDER, i, m), 0)),
                    pl.BlockSpec((width, hidden), lambda i, m: (slice_at(ORDER, i, m), 0)),
                ],
                out_specs=[pl.BlockSpec((half_rows, hidden), lambda i, m: (0, 0))] * 2,
            ),
            compiler_params=params(32),
            cost_estimate=pl.CostEstimate(
                flops=2 * 2 * half_rows * 4 * width * hidden,
                bytes_accessed=2 * 2 * 4 * width * hidden + 2 * half_rows * 4 * width,
                transcendentals=0,
            ),
        )(me, *x, w_gate, w_up)

        def down_at(i, m):
            return (0, slice_at(ORDER, jnp.minimum(i, 3), m))

        def in_at(i, m):
            return (slice_at(SEND_ORDER, jnp.maximum(i - 4, 0), m), 0)

        mids.append(
            pl.pallas_call(
                mid_kernel,
                out_shape=[bf16(half_rows, hidden)] * 3 + [bf16(half_rows, width)] * 4,
                grid_spec=pltpu.PrefetchScalarGridSpec(
                    num_scalar_prefetch=1,
                    grid=(8,),
                    in_specs=[whole(p) for p in y]
                    + [whole(gate_pre), whole(up_pre)]
                    + [
                        pl.BlockSpec((hidden, width), down_at),
                        pl.BlockSpec((width, hidden), in_at),
                        pl.BlockSpec((width, hidden), in_at),
                    ],
                    out_specs=[pl.BlockSpec((half_rows, hidden), lambda i, m: (0, 0))] * 3
                    + [pl.BlockSpec((half_rows, width), lambda i, m: (0, 0))] * 4,
                    scratch_shapes=[pltpu.VMEM((half_rows, hidden), jnp.float32)],
                ),
                compiler_params=params(40),
                cost_estimate=pl.CostEstimate(
                    flops=3 * 2 * half_rows * 4 * width * hidden,
                    bytes_accessed=3 * 2 * 4 * width * hidden + 2 * 2 * half_rows * 4 * width,
                    transcendentals=half_rows * hidden,
                ),
            )(me, *y, gate_pre, up_pre, w_down, w_gate, w_up)
        )

    far_a = passed_along(mids[0][3], "edp", 1)
    far_b = passed_along(mids[1][3], "edp", -1)

    def added(*terms):
        total = terms[0].astype(jnp.float32)
        for term in terms[1:]:
            total = total + term.astype(jnp.float32)
        return total.astype(jnp.bfloat16)

    from_left_a = passed_along(added(mids[0][4], far_a), "edp", 1)
    from_right_a = passed_along(mids[0][5], "edp", -1)
    from_right_b = passed_along(added(mids[1][5], far_b), "edp", -1)
    from_left_b = passed_along(mids[1][4], "edp", 1)
    slot_a = added(mids[0][6], from_left_a, from_right_a)
    slot_b = added(mids[1][6], from_left_b, from_right_b)

    back_a = passed_along(to_experts(slot_a), "section", -1)
    back_b = passed_along(to_experts(slot_b), "section", -1)

    def row_at(i, m):
        return (slice_at(ORDER, i, m), 0)

    def column_at(i, m):
        return (0, slice_at(ORDER, i, m))

    pieces = (*xs[0], *xs[1], *ys[0], *ys[1])
    smalls = (mids[0][0], mids[1][0], mids[0][1], mids[1][1], mids[0][2], mids[1][2])
    grad_gate, grad_up, grad_down = pl.pallas_call(
        grad_kernel,
        out_shape=[bf16(4 * width, hidden)] * 2 + [bf16(hidden, 4 * width)],
        grid_spec=pltpu.PrefetchScalarGridSpec(
            num_scalar_prefetch=1,
            grid=(4,),
            in_specs=[whole(p) for p in pieces + smalls],
            out_specs=[
                pl.BlockSpec((width, hidden), row_at),
                pl.BlockSpec((width, hidden), row_at),
                pl.BlockSpec((hidden, width), column_at),
            ],
        ),
        compiler_params=params(48),
        cost_estimate=pl.CostEstimate(
            flops=3 * 2 * 2 * half_rows * 4 * width * hidden,
            bytes_accessed=3 * 2 * 4 * width * hidden + 4 * 2 * half_rows * 4 * width,
            transcendentals=0,
        ),
    )(me, *pieces, *smalls)

    grad_prev = pl.pallas_call(
        combine_kernel,
        out_shape=bf16(token_count, width),
        compiler_params=params(16),
    )(*choice, back_a, back_b)
    return (grad_prev[None], grad_gate[None, None], grad_up[None, None], grad_down[None, None])


def solution(mesh):
    placed = (
        P("section", "ep", "edp"),
        P("section", "ep", "edp"),
        P("section", "ep", None),
        P("section", "ep", None),
        P("section", "ep", None, "edp"),
        P("section", "ep", None, "edp"),
        P("section", "ep", "edp", None),
    )
    return jax.shard_map(
        body,
        mesh=mesh,
        in_specs=placed,
        out_specs=(
            P("section", "ep", "edp"),
            P("section", "ep", None, "edp"),
            P("section", "ep", None, "edp"),
            P("section", "ep", "edp", None),
        ),
        check_vma=False,
    )
```

```python
import jax
import jax.numpy as jnp
from jax import lax
from jax.experimental import pallas as pl
from jax.experimental.pallas import tpu as pltpu
from jax.sharding import PartitionSpec as P

EXPERTS = 160
TOP = 6
CAP = 24
MIB = 1 << 20


def passed_along(array, axis, by):
    length = lax.axis_size(axis)
    return lax.ppermute(array, axis, [(i, (i + by) % length) for i in range(length)])


def contract(left, right, left_dim, right_dim):
    return lax.dot_general(
        left,
        right,
        (((left_dim,), (right_dim,)), ((), ())),
        preferred_element_type=jnp.float32,
    )


def slot_choice(routes_ref, gates_ref, ep_count):
    token_count = routes_ref.shape[1]
    shape = (ep_count * CAP, token_count)
    slot = lax.broadcasted_iota(jnp.int32, (shape[0], 1), 0)
    expert = slot // CAP
    place = slot - expert * CAP
    wanted = expert * (EXPERTS // ep_count)
    named = jnp.zeros(shape, jnp.float32)
    gate = jnp.zeros(shape, jnp.float32)
    for k in range(TOP):
        hit = routes_ref[k : k + 1, :] == wanted
        named = jnp.where(hit, 1.0, named)
        if gates_ref is not None:
            gate = jnp.where(hit, gates_ref[k : k + 1, :].astype(jnp.float32), gate)
    before = lax.broadcasted_iota(jnp.int32, (token_count, token_count), 0) < (
        lax.broadcasted_iota(jnp.int32, (token_count, token_count), 1)
    )
    earlier = contract(
        named.astype(jnp.bfloat16), jnp.where(before, 1.0, 0.0).astype(jnp.bfloat16), 1, 0
    )
    chosen = (named > 0.0) & (earlier == place.astype(jnp.float32))
    one = jnp.where(chosen, 1.0, 0.0).astype(jnp.bfloat16)
    if gates_ref is None:
        return one, None
    return one, jnp.where(chosen, gate, 0.0).astype(jnp.bfloat16)


def rows_at(ref, index, count):
    return ref[pl.ds(pl.multiple_of(index * count, 128), count), :]


def columns_at(ref, index, count):
    return ref[:, pl.ds(pl.multiple_of(index * count, 128), count)]


def send_x_kernel(ep_count, routes_ref, gates_ref, x_ref, out_ref, gated_ref):
    one, gated_ref[...] = slot_choice(routes_ref, gates_ref, ep_count)
    out_ref[...] = contract(one, x_ref[...], 1, 0).astype(jnp.bfloat16)


def send_y_kernel(gated_ref, dy_ref, out_ref):
    out_ref[...] = contract(gated_ref[...], dy_ref[...], 1, 0).astype(jnp.bfloat16)


def pre_kernel(ep_count, me_ref, routes_ref, x0, x1, x2, wg_ref, wu_ref, gate_ref, up_ref, choice_ref):
    width = x0.shape[1]
    for offset, x in zip(ORDER, (x0, x1, x2)):
        at = lax.rem(me_ref[0] + offset, 4)
        gate = contract(x[...], rows_at(wg_ref, at, width), 1, 0)
        up = contract(x[...], rows_at(wu_ref, at, width), 1, 0)
        if x is x0:
            gate_ref[...] = gate
            up_ref[...] = up
        else:
            gate_ref[...] += gate
            up_ref[...] += up
    choice_ref[...], _ = slot_choice(routes_ref, None, ep_count)


def back_kernel(me_ref, y0, y2, wd_ref, back_ref):
    width = y0.shape[1]
    back_ref[...] = contract(y0[...], columns_at(wd_ref, me_ref[0], width), 1, 1)
    back_ref[...] += contract(y2[...], columns_at(wd_ref, lax.rem(me_ref[0] + 1, 4), width), 1, 1)


def mid_kernel(
    me_ref, x3, y1, y3, gate_ref, up_ref, back_ref, wg_ref, wu_ref, wd_ref,
    dg_ref, du_ref, gh_ref, p0_ref, p1_ref,
):
    width = x3.shape[1]
    left = lax.rem(me_ref[0] + 3, 4)
    far = lax.rem(me_ref[0] + 2, 4)
    wg = rows_at(wg_ref, far, width)
    wu = rows_at(wu_ref, far, width)
    gate_pre = gate_ref[...] + contract(x3[...], wg, 1, 0)
    up_pre = up_ref[...] + contract(x3[...], wu, 1, 0)
    d_hidden = (
        back_ref[...]
        + contract(y1[...], columns_at(wd_ref, left, width), 1, 1)
        + contract(y3[...], columns_at(wd_ref, far, width), 1, 1)
    )
    sigmoid = jax.nn.sigmoid(gate_pre)
    swish = gate_pre * sigmoid
    dg = (d_hidden * up_pre * sigmoid * (1.0 + gate_pre * (1.0 - sigmoid))).astype(jnp.bfloat16)
    du = (d_hidden * swish).astype(jnp.bfloat16)
    dg_ref[...] = dg
    du_ref[...] = du
    gh_ref[...] = (swish * up_pre).astype(jnp.bfloat16)
    half = width // 2
    for h, p_ref in enumerate((p0_ref, p1_ref)):
        rows = slice(h * half, (h + 1) * half)
        p_ref[...] = (contract(dg, wg[rows], 1, 1) + contract(du, wu[rows], 1, 1)).astype(
            jnp.bfloat16
        )


def part_kernel(me_ref, dg_ref, du_ref, wg_ref, wu_ref, r0_ref, r1_ref, l0_ref, l1_ref, own_ref):
    width = own_ref.shape[1]
    half = width // 2
    for offset, outs in ((1, (r0_ref, r1_ref)), (3, (l0_ref, l1_ref)), (0, (own_ref,))):
        at = lax.rem(me_ref[0] + offset, 4)
        wg = rows_at(wg_ref, at, width)
        wu = rows_at(wu_ref, at, width)
        part = contract(dg_ref[...], wg, 1, 1) + contract(du_ref[...], wu, 1, 1)
        part = part.astype(jnp.bfloat16)
        if len(outs) == 1:
            own_ref[...] = part
        else:
            outs[0][...] = part[:, :half]
            outs[1][...] = part[:, half:]


def sum_kernel(own_ref, l0_ref, l1_ref, r0_ref, r1_ref, out_ref):
    half = l0_ref.shape[1]
    rows = own_ref.shape[0]
    for h, (a, b) in enumerate(((l0_ref, r0_ref), (l1_ref, r1_ref))):
        columns = slice(h * half, (h + 1) * half)
        total = own_ref[:, columns].astype(jnp.float32)
        total = total + a[...].astype(jnp.float32) + b[...].astype(jnp.float32)
        total = total.astype(jnp.bfloat16)
        out_ref[:rows, columns] = total
        out_ref[rows:, columns] = total


def grad_kernel(me_ref, *refs):
    x, y = refs[0:4], refs[4:8]
    dg, du, gh, out_g, out_u, out_d = refs[8:]
    step = pl.program_id(0)
    for d in range(4):

        @pl.when(step == d)
        def _(d=d):
            out_g[...] = contract(x[d][...], dg[...], 0, 0).astype(jnp.bfloat16)
            out_u[...] = contract(x[d][...], du[...], 0, 0).astype(jnp.bfloat16)
            out_d[...] = contract(gh[...], y[d][...], 0, 0).astype(jnp.bfloat16)


def combine_kernel(other_ref, choice_ref, rows_ref, out_ref):
    slots = choice_ref.shape[0]
    rows = rows_at(rows_ref, other_ref[0], slots)
    out_ref[...] = contract(choice_ref[...], rows, 0, 0).astype(jnp.bfloat16)


def bf16(*shape):
    return jax.ShapeDtypeStruct(shape, jnp.bfloat16)


def f32(*shape):
    return jax.ShapeDtypeStruct(shape, jnp.float32)


IN_VMEM = pl.BlockSpec(memory_space=pltpu.VMEM)
IN_SMEM = pl.BlockSpec(memory_space=pltpu.SMEM)


def call(kernel, outs, scalars, arrays, products=0):
    return pl.pallas_call(
        kernel,
        out_shape=outs,
        in_specs=[IN_SMEM] * len(scalars) + [IN_VMEM] * len(arrays),
        out_specs=[IN_VMEM] * len(outs),
        compiler_params=pltpu.CompilerParams(vmem_limit_bytes=16 * MIB),
        cost_estimate=pl.CostEstimate(flops=4 * products, bytes_accessed=0, transcendentals=0),
    )(*scalars, *arrays)


ORDER = (0, 3, 1, 2)


def slice_at(step, me_ref):
    offset = jnp.int32(ORDER[3])
    for d in range(3):
        offset = jnp.where(step == d, ORDER[d], offset)
    return lax.rem(me_ref[0] + offset, 4)


def body(tokens, out_grads, gates, routes, w_gate, w_up, w_down):
    ep_count = lax.axis_size("ep")
    token_count, width = tokens.shape[1:]
    rows = ep_count * CAP
    hidden = w_gate.shape[3]
    half = width // 2
    one_slice = rows * width * hidden
    w_gate, w_up, w_down = w_gate[0, 0], w_up[0, 0], w_down[0, 0]
    me = lax.axis_index("edp").astype(jnp.int32).reshape(1)
    other = (1 - lax.axis_index("section")).astype(jnp.int32).reshape(1)

    routes = routes[0].T
    next_routes = passed_along(routes, "section", -1)

    send_x, gated = call(
        lambda *refs: send_x_kernel(ep_count, *refs),
        [bf16(rows, width), bf16(rows, token_count)],
        (),
        (routes, gates[0].T, tokens[0]),
        rows * token_count * (width + token_count),
    )
    (send_y,) = call(
        send_y_kernel, [bf16(rows, width)], (), (gated, out_grads[0]), rows * token_count * width
    )

    def to_experts(array):
        shaped = array.reshape(ep_count, CAP, width)
        return lax.all_to_all(shaped, "ep", split_axis=0, concat_axis=0, tiled=True).reshape(
            rows, width
        )

    own_x = to_experts(send_x)
    send_y, own_x = lax.optimization_barrier((send_y, own_x))
    x_left = passed_along(own_x, "edp", 1)
    x_right = passed_along(own_x, "edp", -1)
    own_y, x_left, x_right = lax.optimization_barrier((to_experts(send_y), x_left, x_right))
    x_far = passed_along(x_left, "edp", 1)
    y_right = passed_along(own_y, "edp", -1)
    y_left = passed_along(own_y, "edp", 1)
    y_far = passed_along(y_right, "edp", -1)

    gate_pre, up_pre, choice = call(
        lambda *refs: pre_kernel(ep_count, *refs),
        [f32(rows, hidden), f32(rows, hidden), bf16(rows, token_count)],
        (me,),
        (next_routes, own_x, x_left, x_right, w_gate, w_up),
        6 * one_slice,
    )
    (back,) = call(
        back_kernel, [f32(rows, hidden)], (me,), (own_y, y_right, w_down), 2 * one_slice
    )
    d_gate, d_up, gated_hidden, far0, far1 = call(
        mid_kernel,
        [bf16(rows, hidden)] * 3 + [bf16(rows, half)] * 2,
        (me,),
        (x_far, y_left, y_far, gate_pre, up_pre, back, w_gate, w_up, w_down),
        6 * one_slice,
    )
    far0 = passed_along(far0, "edp", 1)
    far1 = passed_along(far1, "edp", -1)
    right0, right1, left0, left1, own = call(
        part_kernel,
        [bf16(rows, half)] * 4 + [bf16(rows, width)],
        (me,),
        (d_gate, d_up, w_gate, w_up),
        6 * one_slice,
    )
    d_gate, d_up, gated_hidden, own = lax.optimization_barrier((d_gate, d_up, gated_hidden, own))

    def added(a, b):
        return (a.astype(jnp.float32) + b.astype(jnp.float32)).astype(jnp.bfloat16)

    from_left1 = passed_along(right1, "edp", 1)
    from_right0 = passed_along(left0, "edp", -1)
    from_left0 = passed_along(added(right0, far0), "edp", 1)
    from_right1 = passed_along(added(left1, far1), "edp", -1)

    x, y = (own_x, x_left, x_right, x_far), (own_y, y_left, y_right, y_far)
    smalls = (d_gate, d_up, gated_hidden)
    grad_gate, grad_up, grad_down = pl.pallas_call(
        grad_kernel,
        out_shape=[bf16(4 * width, hidden)] * 2 + [bf16(hidden, 4 * width)],
        grid_spec=pltpu.PrefetchScalarGridSpec(
            num_scalar_prefetch=1,
            grid=(4,),
            in_specs=[IN_VMEM] * 11,
            out_specs=[
                pl.BlockSpec((width, hidden), lambda i, m: (slice_at(i, m), 0)),
                pl.BlockSpec((width, hidden), lambda i, m: (slice_at(i, m), 0)),
                pl.BlockSpec((hidden, width), lambda i, m: (0, slice_at(i, m))),
            ],
        ),
        compiler_params=pltpu.CompilerParams(vmem_limit_bytes=16 * MIB),
        cost_estimate=pl.CostEstimate(
            flops=4 * 12 * one_slice, bytes_accessed=0, transcendentals=0
        ),
    )(me, *x, *y, *smalls)
    from_left0, from_right1, grad_gate, grad_up, grad_down = lax.optimization_barrier(
        (from_left0, from_right1, grad_gate, grad_up, grad_down)
    )

    (summed,) = call(
        sum_kernel,
        [bf16(2 * rows, width)],
        (),
        (own, from_left0, from_left1, from_right0, from_right1),
    )
    returned = lax.all_to_all(
        summed.reshape(2 * ep_count, CAP, width),
        ("section", "ep"),
        split_axis=0,
        concat_axis=0,
        tiled=True,
    ).reshape(2 * rows, width)
    (grad_prev,) = call(
        combine_kernel,
        [bf16(token_count, width)],
        (other,),
        (choice, returned),
        rows * token_count * width,
    )
    return (grad_prev[None], grad_gate[None, None], grad_up[None, None], grad_down[None, None])


def solution(mesh):
    placed = (
        P("section", "ep", "edp"),
        P("section", "ep", "edp"),
        P("section", "ep", None),
        P("section", "ep", None),
        P("section", "ep", None, "edp"),
        P("section", "ep", None, "edp"),
        P("section", "ep", "edp", None),
    )
    return jax.shard_map(
        body,
        mesh=mesh,
        in_specs=placed,
        out_specs=(
            P("section", "ep", "edp"),
            P("section", "ep", None, "edp"),
            P("section", "ep", None, "edp"),
            P("section", "ep", "edp", None),
        ),
        check_vma=False,
    )
```

```python
import jax
import jax.numpy as jnp
from jax import lax
from jax.experimental import pallas as pl
from jax.experimental.pallas import tpu as pltpu
from jax.sharding import PartitionSpec as P

EXPERTS = 160
TOP = 6
CAP = 24
MIB = 1 << 20


def passed_along(array, axis, by):
    length = lax.axis_size(axis)
    return lax.ppermute(array, axis, [(i, (i + by) % length) for i in range(length)])


def contract(left, right, left_dim, right_dim):
    return lax.dot_general(
        left,
        right,
        (((left_dim,), (right_dim,)), ((), ())),
        preferred_element_type=jnp.float32,
    )


def slot_choice(routes_ref, gates_ref, ep_count):
    token_count = routes_ref.shape[1]
    shape = (ep_count * CAP, token_count)
    slot = lax.broadcasted_iota(jnp.int32, (shape[0], 1), 0)
    expert = slot // CAP
    place = slot - expert * CAP
    wanted = expert * (EXPERTS // ep_count)
    named = jnp.zeros(shape, jnp.float32)
    gate = jnp.zeros(shape, jnp.float32)
    for k in range(TOP):
        hit = routes_ref[k : k + 1, :] == wanted
        named = jnp.where(hit, 1.0, named)
        if gates_ref is not None:
            gate = jnp.where(hit, gates_ref[k : k + 1, :].astype(jnp.float32), gate)
    before = lax.broadcasted_iota(jnp.int32, (token_count, token_count), 0) < (
        lax.broadcasted_iota(jnp.int32, (token_count, token_count), 1)
    )
    earlier = contract(
        named.astype(jnp.bfloat16), jnp.where(before, 1.0, 0.0).astype(jnp.bfloat16), 1, 0
    )
    chosen = (named > 0.0) & (earlier == place.astype(jnp.float32))
    one = jnp.where(chosen, 1.0, 0.0).astype(jnp.bfloat16)
    if gates_ref is None:
        return one, None
    return one, jnp.where(chosen, gate, 0.0).astype(jnp.bfloat16)


def rows_at(ref, index, count):
    return ref[pl.ds(pl.multiple_of(index * count, 128), count), :]


def columns_at(ref, index, count):
    return ref[:, pl.ds(pl.multiple_of(index * count, 128), count)]


def send_x_kernel(ep_count, routes_ref, gates_ref, x_ref, out_ref, gated_ref):
    one, gated_ref[...] = slot_choice(routes_ref, gates_ref, ep_count)
    out_ref[...] = contract(one, x_ref[...], 1, 0).astype(jnp.bfloat16)


def send_y_kernel(gated_ref, dy_ref, out_ref):
    out_ref[...] = contract(gated_ref[...], dy_ref[...], 1, 0).astype(jnp.bfloat16)


def pre_kernel(ep_count, me_ref, routes_ref, x0, x1, x2, wg_ref, wu_ref, gate_ref, up_ref, choice_ref):
    width = x0.shape[1]
    for offset, x in zip(ORDER, (x0, x1, x2)):
        at = lax.rem(me_ref[0] + offset, 4)
        gate = contract(x[...], rows_at(wg_ref, at, width), 1, 0)
        up = contract(x[...], rows_at(wu_ref, at, width), 1, 0)
        if x is x0:
            gate_ref[...] = gate
            up_ref[...] = up
        else:
            gate_ref[...] += gate
            up_ref[...] += up
    choice_ref[...], _ = slot_choice(routes_ref, None, ep_count)


def back_kernel(me_ref, y0, y1, y2, wd_ref, back_ref):
    width = y0.shape[1]
    for offset, y in zip(ORDER, (y0, y1, y2)):
        at = lax.rem(me_ref[0] + offset, 4)
        back = contract(y[...], columns_at(wd_ref, at, width), 1, 1)
        if y is y0:
            back_ref[...] = back
        else:
            back_ref[...] += back


def mid_kernel(
    me_ref, x30, x31, y30, y31, gate_ref, up_ref, back_ref, wg_ref, wu_ref, wd_ref,
    dg_ref, du_ref, gh_ref, p0_ref, p1_ref,
):
    half = x30.shape[1]
    width = 2 * half
    far = lax.rem(me_ref[0] + 2, 4)
    wg = rows_at(wg_ref, far, width)
    wu = rows_at(wu_ref, far, width)
    wd = columns_at(wd_ref, far, width)
    gate_pre = gate_ref[...]
    up_pre = up_ref[...]
    d_hidden = back_ref[...]
    for h, (x, y) in enumerate(((x30, y30), (x31, y31))):
        span = slice(h * half, (h + 1) * half)
        gate_pre += contract(x[...], wg[span], 1, 0)
        up_pre += contract(x[...], wu[span], 1, 0)
        d_hidden += contract(y[...], wd[:, span], 1, 1)
    sigmoid = jax.nn.sigmoid(gate_pre)
    swish = gate_pre * sigmoid
    dg = (d_hidden * up_pre * sigmoid * (1.0 + gate_pre * (1.0 - sigmoid))).astype(jnp.bfloat16)
    du = (d_hidden * swish).astype(jnp.bfloat16)
    dg_ref[...] = dg
    du_ref[...] = du
    gh_ref[...] = (swish * up_pre).astype(jnp.bfloat16)
    for h, p_ref in enumerate((p0_ref, p1_ref)):
        rows = slice(h * half, (h + 1) * half)
        p_ref[...] = (contract(dg, wg[rows], 1, 1) + contract(du, wu[rows], 1, 1)).astype(
            jnp.bfloat16
        )


def part_kernel(me_ref, dg_ref, du_ref, wg_ref, wu_ref, r0_ref, r1_ref, l0_ref, l1_ref, own_ref):
    width = own_ref.shape[1]
    half = width // 2
    for offset, outs in ((1, (r0_ref, r1_ref)), (3, (l0_ref, l1_ref)), (0, (own_ref,))):
        at = lax.rem(me_ref[0] + offset, 4)
        wg = rows_at(wg_ref, at, width)
        wu = rows_at(wu_ref, at, width)
        part = contract(dg_ref[...], wg, 1, 1) + contract(du_ref[...], wu, 1, 1)
        part = part.astype(jnp.bfloat16)
        if len(outs) == 1:
            own_ref[...] = part
        else:
            outs[0][...] = part[:, :half]
            outs[1][...] = part[:, half:]


def sum_kernel(own_ref, l0_ref, l1_ref, r0_ref, r1_ref, out_ref):
    half = l0_ref.shape[1]
    rows = own_ref.shape[0]
    for h, (a, b) in enumerate(((l0_ref, r0_ref), (l1_ref, r1_ref))):
        columns = slice(h * half, (h + 1) * half)
        total = own_ref[:, columns].astype(jnp.float32)
        total = total + a[...].astype(jnp.float32) + b[...].astype(jnp.float32)
        total = total.astype(jnp.bfloat16)
        out_ref[:rows, columns] = total
        out_ref[rows:, columns] = total


def grad_kernel(me_ref, *refs):
    x, y = refs[0:5], refs[5:10]
    dg, du, gh, out_g, out_u, out_d = refs[10:]
    step = pl.program_id(0)
    for d in range(4):

        @pl.when(step == d)
        def _(d=d):
            for n, (x_ref, y_ref) in enumerate(zip(x[d : d + 1 + d // 3], y[d : d + 1 + d // 3])):
                count = x_ref.shape[1]
                span = slice(n * count, (n + 1) * count)
                out_g[span, :] = contract(x_ref[...], dg[...], 0, 0).astype(jnp.bfloat16)
                out_u[span, :] = contract(x_ref[...], du[...], 0, 0).astype(jnp.bfloat16)
                out_d[:, span] = contract(gh[...], y_ref[...], 0, 0).astype(jnp.bfloat16)


def combine_kernel(other_ref, choice_ref, rows_ref, out_ref):
    slots = choice_ref.shape[0]
    rows = rows_at(rows_ref, other_ref[0], slots)
    out_ref[...] = contract(choice_ref[...], rows, 0, 0).astype(jnp.bfloat16)


def bf16(*shape):
    return jax.ShapeDtypeStruct(shape, jnp.bfloat16)


def f32(*shape):
    return jax.ShapeDtypeStruct(shape, jnp.float32)


IN_VMEM = pl.BlockSpec(memory_space=pltpu.VMEM)
IN_SMEM = pl.BlockSpec(memory_space=pltpu.SMEM)


def whole(array):
    return pl.BlockSpec(array.shape, lambda *_: (0,) * len(array.shape), pipeline_mode=pl.Buffered(1))


def in_hbm(array):
    return pltpu.with_memory_space_constraint(array, pltpu.HBM)


def call(kernel, outs, scalars, arrays, products=0):
    return pl.pallas_call(
        kernel,
        out_shape=outs,
        in_specs=[IN_SMEM] * len(scalars) + [IN_VMEM] * len(arrays),
        out_specs=[IN_VMEM] * len(outs),
        compiler_params=pltpu.CompilerParams(vmem_limit_bytes=16 * MIB),
        cost_estimate=pl.CostEstimate(flops=4 * products, bytes_accessed=0, transcendentals=0),
    )(*scalars, *arrays)


ORDER = (0, 3, 1, 2)


def slice_at(step, me_ref):
    offset = jnp.int32(ORDER[3])
    for d in range(3):
        offset = jnp.where(step == d, ORDER[d], offset)
    return lax.rem(me_ref[0] + offset, 4)


def body(tokens, out_grads, gates, routes, w_gate, w_up, w_down):
    ep_count = lax.axis_size("ep")
    token_count, width = tokens.shape[1:]
    rows = ep_count * CAP
    hidden = w_gate.shape[3]
    half = width // 2
    one_slice = rows * width * hidden
    w_gate, w_up, w_down = w_gate[0, 0], w_up[0, 0], w_down[0, 0]
    me = lax.axis_index("edp").astype(jnp.int32).reshape(1)
    other = (1 - lax.axis_index("section")).astype(jnp.int32).reshape(1)

    routes, me, other = lax.optimization_barrier((routes[0].T, me, other))
    next_routes = passed_along(routes, "section", -1)

    send_x, gated = call(
        lambda *refs: send_x_kernel(ep_count, *refs),
        [bf16(rows, width), bf16(rows, token_count)],
        (),
        (routes, gates[0].T, tokens[0]),
        rows * token_count * (width + token_count),
    )
    (send_y,) = call(
        send_y_kernel, [bf16(rows, width)], (), (gated, out_grads[0]), rows * token_count * width
    )

    def to_experts(array):
        shaped = array.reshape(ep_count, CAP, width)
        return lax.all_to_all(shaped, "ep", split_axis=0, concat_axis=0, tiled=True).reshape(
            rows, width
        )

    own_x = to_experts(send_x)
    send_y, own_x = lax.optimization_barrier((send_y, own_x))
    x_left = passed_along(own_x, "edp", 1)
    x_right = passed_along(own_x, "edp", -1)
    own_y, x_left, x_right = lax.optimization_barrier((to_experts(send_y), x_left, x_right))
    x_far0 = passed_along(x_left[:, :half], "edp", 1)
    x_far1 = passed_along(x_right[:, half:], "edp", -1)
    y_right = passed_along(own_y, "edp", -1)
    y_left = passed_along(own_y, "edp", 1)

    gate_pre, up_pre, choice = call(
        lambda *refs: pre_kernel(ep_count, *refs),
        [f32(rows, hidden), f32(rows, hidden), bf16(rows, token_count)],
        (me,),
        (next_routes, own_x, x_left, x_right, w_gate, w_up),
        6 * one_slice,
    )
    y_left, y_right, gate_pre, up_pre, choice = lax.optimization_barrier(
        (y_left, y_right, gate_pre, up_pre, choice)
    )
    y_far0 = passed_along(y_left[:, :half], "edp", 1)
    y_far1 = passed_along(y_right[:, half:], "edp", -1)
    (back,) = call(
        back_kernel,
        [f32(rows, hidden)],
        (me,),
        (own_y, y_left, y_right, w_down),
        3 * one_slice,
    )
    d_gate, d_up, gated_hidden, far0, far1 = call(
        mid_kernel,
        [bf16(rows, hidden)] * 3 + [bf16(rows, half)] * 2,
        (me,),
        (x_far0, x_far1, y_far0, y_far1, gate_pre, up_pre, back, w_gate, w_up, w_down),
        5 * one_slice,
    )
    far0 = passed_along(far0, "edp", 1)
    far1 = passed_along(far1, "edp", -1)
    right0, right1, left0, left1, own = call(
        part_kernel,
        [bf16(rows, half)] * 4 + [bf16(rows, width)],
        (me,),
        (d_gate, d_up, w_gate, w_up),
        6 * one_slice,
    )

    def added(a, b):
        return (a.astype(jnp.float32) + b.astype(jnp.float32)).astype(jnp.bfloat16)

    from_left1 = passed_along(right1, "edp", 1)
    from_right0 = passed_along(left0, "edp", -1)
    from_left0 = passed_along(added(right0, far0), "edp", 1)
    from_right1 = passed_along(added(left1, far1), "edp", -1)

    (summed,) = call(
        sum_kernel,
        [bf16(2 * rows, width)],
        (),
        (own, from_left0, from_left1, from_right0, from_right1),
    )
    summed, d_gate, d_up, gated_hidden = lax.optimization_barrier(
        (summed, d_gate, d_up, gated_hidden)
    )
    x = (own_x, x_left, x_right, x_far0, x_far1)
    y = (own_y, y_left, y_right, y_far0, y_far1)
    smalls = (d_gate, d_up, gated_hidden)
    grad_gate, grad_up, grad_down = pl.pallas_call(
        grad_kernel,
        out_shape=[bf16(4 * width, hidden)] * 2 + [bf16(hidden, 4 * width)],
        grid_spec=pltpu.PrefetchScalarGridSpec(
            num_scalar_prefetch=1,
            grid=(4,),
            in_specs=[whole(a) for a in (*x, *y, *smalls)],
            out_specs=[
                pl.BlockSpec((width, hidden), lambda i, m: (slice_at(i, m), 0)),
                pl.BlockSpec((width, hidden), lambda i, m: (slice_at(i, m), 0)),
                pl.BlockSpec((hidden, width), lambda i, m: (0, slice_at(i, m))),
            ],
        ),
        compiler_params=pltpu.CompilerParams(vmem_limit_bytes=28 * MIB),
        cost_estimate=pl.CostEstimate(
            flops=4 * 12 * one_slice, bytes_accessed=0, transcendentals=0
        ),
    )(me, *(in_hbm(a) for a in (*x, *y, *smalls)))
    returned = lax.all_to_all(
        summed.reshape(2 * ep_count, CAP, width),
        ("section", "ep"),
        split_axis=0,
        concat_axis=0,
        tiled=True,
    ).reshape(2 * rows, width)
    (grad_prev,) = call(
        combine_kernel,
        [bf16(token_count, width)],
        (other,),
        (choice, returned),
        rows * token_count * width,
    )
    return (grad_prev[None], grad_gate[None, None], grad_up[None, None], grad_down[None, None])


def solution(mesh):
    placed = (
        P("section", "ep", "edp"),
        P("section", "ep", "edp"),
        P("section", "ep", None),
        P("section", "ep", None),
        P("section", "ep", None, "edp"),
        P("section", "ep", None, "edp"),
        P("section", "ep", "edp", None),
    )
    return jax.shard_map(
        body,
        mesh=mesh,
        in_specs=placed,
        out_specs=(
            P("section", "ep", "edp"),
            P("section", "ep", None, "edp"),
            P("section", "ep", None, "edp"),
            P("section", "ep", "edp", None),
        ),
        check_vma=False,
    )
```

```python
import jax
import jax.numpy as jnp
from jax import lax
from jax.experimental import pallas as pl
from jax.experimental.pallas import tpu as pltpu
from jax.sharding import PartitionSpec as P

EXPERTS = 160
TOP = 6
CAP = 24
MIB = 1 << 20


def passed_along(array, axis, by):
    length = lax.axis_size(axis)
    return lax.ppermute(array, axis, [(i, (i + by) % length) for i in range(length)])


def contract(left, right, left_dim, right_dim):
    return lax.dot_general(
        left,
        right,
        (((left_dim,), (right_dim,)), ((), ())),
        preferred_element_type=jnp.float32,
    )


def slot_choice(routes_ref, gates_ref, ep_count):
    token_count = routes_ref.shape[1]
    shape = (ep_count * CAP, token_count)
    slot = lax.broadcasted_iota(jnp.int32, (shape[0], 1), 0)
    expert = slot // CAP
    place = slot - expert * CAP
    wanted = expert * (EXPERTS // ep_count)
    named = jnp.zeros(shape, jnp.float32)
    gate = jnp.zeros(shape, jnp.float32)
    for k in range(TOP):
        hit = routes_ref[k : k + 1, :] == wanted
        named = jnp.where(hit, 1.0, named)
        if gates_ref is not None:
            gate = jnp.where(hit, gates_ref[k : k + 1, :].astype(jnp.float32), gate)
    before = lax.broadcasted_iota(jnp.int32, (token_count, token_count), 0) < (
        lax.broadcasted_iota(jnp.int32, (token_count, token_count), 1)
    )
    earlier = contract(
        named.astype(jnp.bfloat16), jnp.where(before, 1.0, 0.0).astype(jnp.bfloat16), 1, 0
    )
    chosen = (named > 0.0) & (earlier == place.astype(jnp.float32))
    one = jnp.where(chosen, 1.0, 0.0).astype(jnp.bfloat16)
    if gates_ref is None:
        return one, None
    return one, jnp.where(chosen, gate, 0.0).astype(jnp.bfloat16)


def rows_at(ref, index, count):
    return ref[pl.ds(pl.multiple_of(index * count, 128), count), :]


def columns_at(ref, index, count):
    return ref[:, pl.ds(pl.multiple_of(index * count, 128), count)]


def send_x_kernel(ep_count, routes_ref, gates_ref, x_ref, out_ref, gated_ref):
    one, gated_ref[...] = slot_choice(routes_ref, gates_ref, ep_count)
    out_ref[...] = contract(one, x_ref[...], 1, 0).astype(jnp.bfloat16)


def send_y_kernel(gated_ref, dy_ref, out_ref):
    out_ref[...] = contract(gated_ref[...], dy_ref[...], 1, 0).astype(jnp.bfloat16)


def pre_kernel(ep_count, me_ref, routes_ref, x0, x1, x2, wg_ref, wu_ref, gate_ref, up_ref, choice_ref):
    width = x0.shape[1]
    for offset, x in zip(ORDER, (x0, x1, x2)):
        at = lax.rem(me_ref[0] + offset, 4)
        gate = contract(x[...], rows_at(wg_ref, at, width), 1, 0)
        up = contract(x[...], rows_at(wu_ref, at, width), 1, 0)
        if x is x0:
            gate_ref[...] = gate
            up_ref[...] = up
        else:
            gate_ref[...] += gate
            up_ref[...] += up
    choice_ref[...], _ = slot_choice(routes_ref, None, ep_count)


def back_kernel(me_ref, y0, y1, y2, wd_ref, back_ref):
    width = y0.shape[1]
    for offset, y in zip(ORDER, (y0, y1, y2)):
        at = lax.rem(me_ref[0] + offset, 4)
        back = contract(y[...], columns_at(wd_ref, at, width), 1, 1)
        if y is y0:
            back_ref[...] = back
        else:
            back_ref[...] += back


def mid_kernel(
    me_ref, x30, x31, y30, y31, gate_ref, up_ref, back_ref, wg_ref, wu_ref, wd_ref,
    dg_ref, du_ref, gh_ref, p0_ref, p1_ref,
):
    half = x30.shape[1]
    width = 2 * half
    far = lax.rem(me_ref[0] + 2, 4)
    wg = rows_at(wg_ref, far, width)
    wu = rows_at(wu_ref, far, width)
    wd = columns_at(wd_ref, far, width)
    gate_pre = gate_ref[...]
    up_pre = up_ref[...]
    d_hidden = back_ref[...]
    for h, (x, y) in enumerate(((x30, y30), (x31, y31))):
        span = slice(h * half, (h + 1) * half)
        gate_pre += contract(x[...], wg[span], 1, 0)
        up_pre += contract(x[...], wu[span], 1, 0)
        d_hidden += contract(y[...], wd[:, span], 1, 1)
    sigmoid = jax.nn.sigmoid(gate_pre)
    swish = gate_pre * sigmoid
    dg = (d_hidden * up_pre * sigmoid * (1.0 + gate_pre * (1.0 - sigmoid))).astype(jnp.bfloat16)
    du = (d_hidden * swish).astype(jnp.bfloat16)
    dg_ref[...] = dg
    du_ref[...] = du
    gh_ref[...] = (swish * up_pre).astype(jnp.bfloat16)
    for p_ref, rows in ((p0_ref, slice(0, SHIFTED)), (p1_ref, slice(SHIFTED, width))):
        p_ref[...] = (contract(dg, wg[rows], 1, 1) + contract(du, wu[rows], 1, 1)).astype(
            jnp.bfloat16
        )


def part_kernel(me_ref, dg_ref, du_ref, wg_ref, wu_ref, r0_ref, r1_ref, l0_ref, l1_ref, own_ref):
    width = own_ref.shape[1]
    for offset, outs in ((3, (l0_ref, l1_ref)), (1, (r0_ref, r1_ref)), (0, (own_ref,))):
        at = lax.rem(me_ref[0] + offset, 4)
        wg = rows_at(wg_ref, at, width)
        wu = rows_at(wu_ref, at, width)
        part = contract(dg_ref[...], wg, 1, 1) + contract(du_ref[...], wu, 1, 1)
        part = part.astype(jnp.bfloat16)
        if len(outs) == 1:
            own_ref[...] = part
        else:
            outs[0][...] = part[:, :SHIFTED]
            outs[1][...] = part[:, SHIFTED:]


def sum_kernel(own_ref, l_ref, r_ref, out_ref):
    total = own_ref[:, :SHIFTED].astype(jnp.float32)
    total = total + l_ref[...].astype(jnp.float32) + r_ref[...].astype(jnp.float32)
    out_ref[...] = total.astype(jnp.bfloat16)


def pack_kernel(section_ref, own_ref, l_ref, r_ref, shifted_ref, out_ref):
    rows = own_ref.shape[0]
    here = pl.multiple_of(section_ref[0] * rows, 128)
    there = pl.multiple_of((1 - section_ref[0]) * rows, 128)
    total = own_ref[:, SHIFTED:].astype(jnp.float32)
    total = total + l_ref[...].astype(jnp.float32) + r_ref[...].astype(jnp.float32)
    out_ref[pl.ds(there, rows), :] = total.astype(jnp.bfloat16)
    out_ref[pl.ds(here, rows), :SHIFTED] = shifted_ref[...]
    unused = out_ref.shape[1] - SHIFTED
    if unused:
        out_ref[pl.ds(here, rows), SHIFTED:] = jnp.zeros((rows, unused), jnp.bfloat16)


def grad_kernel(me_ref, *refs):
    x, y = refs[0:5], refs[5:10]
    dg, du, gh, out_g, out_u, out_d = refs[10:]
    step = pl.program_id(0)
    for d in range(4):

        @pl.when(step == d)
        def _(d=d):
            for n, (x_ref, y_ref) in enumerate(zip(x[d : d + 1 + d // 3], y[d : d + 1 + d // 3])):
                count = x_ref.shape[1]
                span = slice(n * count, (n + 1) * count)
                out_g[span, :] = contract(x_ref[...], dg[...], 0, 0).astype(jnp.bfloat16)
                out_u[span, :] = contract(x_ref[...], du[...], 0, 0).astype(jnp.bfloat16)
                out_d[:, span] = contract(gh[...], y_ref[...], 0, 0).astype(jnp.bfloat16)


def combine_kernel(section_ref, choice_ref, rows_ref, out_ref):
    slots = choice_ref.shape[0]
    shifted = rows_at(rows_ref, section_ref[0], slots)[:, :SHIFTED]
    out_ref[:, :SHIFTED] = contract(choice_ref[...], shifted, 0, 0).astype(jnp.bfloat16)
    rest = rows_at(rows_ref, 1 - section_ref[0], slots)
    out_ref[:, SHIFTED:] = contract(choice_ref[...], rest, 0, 0).astype(jnp.bfloat16)


def bf16(*shape):
    return jax.ShapeDtypeStruct(shape, jnp.bfloat16)


def f32(*shape):
    return jax.ShapeDtypeStruct(shape, jnp.float32)


IN_VMEM = pl.BlockSpec(memory_space=pltpu.VMEM)
IN_SMEM = pl.BlockSpec(memory_space=pltpu.SMEM)


def whole(array):
    return pl.BlockSpec(array.shape, lambda *_: (0,) * len(array.shape), pipeline_mode=pl.Buffered(1))


def in_hbm(array):
    return pltpu.with_memory_space_constraint(array, pltpu.HBM)


def call(kernel, outs, scalars, arrays, products=0):
    return pl.pallas_call(
        kernel,
        out_shape=outs,
        in_specs=[IN_SMEM] * len(scalars) + [IN_VMEM] * len(arrays),
        out_specs=[IN_VMEM] * len(outs),
        compiler_params=pltpu.CompilerParams(vmem_limit_bytes=16 * MIB),
        cost_estimate=pl.CostEstimate(flops=4 * products, bytes_accessed=0, transcendentals=0),
    )(*scalars, *arrays)


SHIFTED = 512
ORDER = (0, 3, 1, 2)


def slice_at(step, me_ref):
    offset = jnp.int32(ORDER[3])
    for d in range(3):
        offset = jnp.where(step == d, ORDER[d], offset)
    return lax.rem(me_ref[0] + offset, 4)


def body(tokens, out_grads, gates, routes, w_gate, w_up, w_down):
    ep_count = lax.axis_size("ep")
    token_count, width = tokens.shape[1:]
    rows = ep_count * CAP
    hidden = w_gate.shape[3]
    half = width // 2
    one_slice = rows * width * hidden
    w_gate, w_up, w_down = w_gate[0, 0], w_up[0, 0], w_down[0, 0]
    me = lax.axis_index("edp").astype(jnp.int32).reshape(1)
    section = lax.axis_index("section").astype(jnp.int32).reshape(1)

    routes, me, section = lax.optimization_barrier((routes[0].T, me, section))
    next_routes = passed_along(routes, "section", -1)

    send_x, gated = call(
        lambda *refs: send_x_kernel(ep_count, *refs),
        [bf16(rows, width), bf16(rows, token_count)],
        (),
        (routes, gates[0].T, tokens[0]),
        rows * token_count * (width + token_count),
    )
    (send_y,) = call(
        send_y_kernel, [bf16(rows, width)], (), (gated, out_grads[0]), rows * token_count * width
    )

    def to_experts(array):
        shaped = array.reshape(ep_count, CAP, width)
        return lax.all_to_all(shaped, "ep", split_axis=0, concat_axis=0, tiled=True).reshape(
            rows, width
        )

    own_x = to_experts(send_x)
    send_y, own_x = lax.optimization_barrier((send_y, own_x))
    x_left = passed_along(own_x, "edp", 1)
    x_right = passed_along(own_x, "edp", -1)
    own_y, x_left, x_right = lax.optimization_barrier((to_experts(send_y), x_left, x_right))
    x_far0 = passed_along(x_left[:, :half], "edp", 1)
    x_far1 = passed_along(x_right[:, half:], "edp", -1)
    y_right = passed_along(own_y, "edp", -1)
    y_left = passed_along(own_y, "edp", 1)

    gate_pre, up_pre, choice = call(
        lambda *refs: pre_kernel(ep_count, *refs),
        [f32(rows, hidden), f32(rows, hidden), bf16(rows, token_count)],
        (me,),
        (next_routes, own_x, x_left, x_right, w_gate, w_up),
        6 * one_slice,
    )
    y_left, y_right, gate_pre, up_pre, choice = lax.optimization_barrier(
        (y_left, y_right, gate_pre, up_pre, choice)
    )
    y_far0 = passed_along(y_left[:, :half], "edp", 1)
    y_far1 = passed_along(y_right[:, half:], "edp", -1)
    (back,) = call(
        back_kernel,
        [f32(rows, hidden)],
        (me,),
        (own_y, y_left, y_right, w_down),
        3 * one_slice,
    )
    parts = [bf16(rows, SHIFTED), bf16(rows, width - SHIFTED)]
    d_gate, d_up, gated_hidden, far0, far1 = call(
        mid_kernel,
        [bf16(rows, hidden)] * 3 + parts,
        (me,),
        (x_far0, x_far1, y_far0, y_far1, gate_pre, up_pre, back, w_gate, w_up, w_down),
        5 * one_slice,
    )
    far0 = passed_along(far0, "edp", 1)
    far1 = passed_along(far1, "edp", -1)
    right0, right1, left0, left1, own = call(
        part_kernel,
        parts * 2 + [bf16(rows, width)],
        (me,),
        (d_gate, d_up, w_gate, w_up),
        6 * one_slice,
    )

    def added(a, b):
        return (a.astype(jnp.float32) + b.astype(jnp.float32)).astype(jnp.bfloat16)

    right0, right1 = lax.optimization_barrier((added(right0, far0), right1))
    from_left0 = passed_along(right0, "edp", 1)
    from_right0 = passed_along(left0, "edp", -1)
    from_left1 = passed_along(right1, "edp", 1)
    from_right1 = passed_along(added(left1, far1), "edp", -1)
    (shifted,) = call(sum_kernel, parts[:1], (), (own, from_left0, from_right0))
    shifted = passed_along(shifted, "section", -1)
    (packed,) = call(
        pack_kernel,
        [bf16(2 * rows, max(SHIFTED, width - SHIFTED))],
        (section,),
        (own, from_left1, from_right1, shifted),
    )
    packed, d_gate, d_up, gated_hidden = lax.optimization_barrier(
        (packed, d_gate, d_up, gated_hidden)
    )
    x = (own_x, x_left, x_right, x_far0, x_far1)
    y = (own_y, y_left, y_right, y_far0, y_far1)
    smalls = (d_gate, d_up, gated_hidden)
    grad_gate, grad_up, grad_down = pl.pallas_call(
        grad_kernel,
        out_shape=[bf16(4 * width, hidden)] * 2 + [bf16(hidden, 4 * width)],
        grid_spec=pltpu.PrefetchScalarGridSpec(
            num_scalar_prefetch=1,
            grid=(4,),
            in_specs=[whole(a) for a in (*x, *y, *smalls)],
            out_specs=[
                pl.BlockSpec((width, hidden), lambda i, m: (slice_at(i, m), 0)),
                pl.BlockSpec((width, hidden), lambda i, m: (slice_at(i, m), 0)),
                pl.BlockSpec((hidden, width), lambda i, m: (0, slice_at(i, m))),
            ],
        ),
        compiler_params=pltpu.CompilerParams(vmem_limit_bytes=28 * MIB),
        cost_estimate=pl.CostEstimate(
            flops=4 * 12 * one_slice, bytes_accessed=0, transcendentals=0
        ),
    )(me, *(in_hbm(a) for a in (*x, *y, *smalls)))
    returned = lax.all_to_all(
        packed.reshape(2 * ep_count, CAP, -1),
        ("section", "ep"),
        split_axis=0,
        concat_axis=0,
        tiled=True,
    ).reshape(2 * rows, -1)
    (grad_prev,) = call(
        combine_kernel,
        [bf16(token_count, width)],
        (section,),
        (choice, returned),
        rows * token_count * width,
    )
    return (grad_prev[None], grad_gate[None, None], grad_up[None, None], grad_down[None, None])


def solution(mesh):
    placed = (
        P("section", "ep", "edp"),
        P("section", "ep", "edp"),
        P("section", "ep", None),
        P("section", "ep", None),
        P("section", "ep", None, "edp"),
        P("section", "ep", None, "edp"),
        P("section", "ep", "edp", None),
    )
    return jax.shard_map(
        body,
        mesh=mesh,
        in_specs=placed,
        out_specs=(
            P("section", "ep", "edp"),
            P("section", "ep", None, "edp"),
            P("section", "ep", None, "edp"),
            P("section", "ep", "edp", None),
        ),
        check_vma=False,
    )
```

```python
import jax
import jax.numpy as jnp
from jax import lax
from jax.experimental import pallas as pl
from jax.experimental.pallas import tpu as pltpu
from jax.sharding import PartitionSpec as P

EXPERTS = 160
TOP = 6
CAP = 24
MIB = 1 << 20


def passed_along(array, axis, by):
    length = lax.axis_size(axis)
    return lax.ppermute(array, axis, [(i, (i + by) % length) for i in range(length)])


def contract(left, right, left_dim, right_dim):
    return lax.dot_general(
        left,
        right,
        (((left_dim,), (right_dim,)), ((), ())),
        preferred_element_type=jnp.float32,
    )


def slot_choice(routes_ref, gates_ref, ep_count):
    token_count = routes_ref.shape[1]
    shape = (ep_count * CAP, token_count)
    slot = lax.broadcasted_iota(jnp.int32, (shape[0], 1), 0)
    expert = slot // CAP
    place = slot - expert * CAP
    wanted = expert * (EXPERTS // ep_count)
    named = jnp.zeros(shape, jnp.float32)
    gate = jnp.zeros(shape, jnp.float32)
    for k in range(TOP):
        hit = routes_ref[k : k + 1, :] == wanted
        named = jnp.where(hit, 1.0, named)
        if gates_ref is not None:
            gate = jnp.where(hit, gates_ref[k : k + 1, :].astype(jnp.float32), gate)
    before = lax.broadcasted_iota(jnp.int32, (token_count, token_count), 0) < (
        lax.broadcasted_iota(jnp.int32, (token_count, token_count), 1)
    )
    earlier = contract(
        named.astype(jnp.bfloat16), jnp.where(before, 1.0, 0.0).astype(jnp.bfloat16), 1, 0
    )
    chosen = (named > 0.0) & (earlier == place.astype(jnp.float32))
    one = jnp.where(chosen, 1.0, 0.0).astype(jnp.bfloat16)
    if gates_ref is None:
        return one, None
    return one, jnp.where(chosen, gate, 0.0).astype(jnp.bfloat16)


def rows_at(ref, index, count):
    return ref[pl.ds(pl.multiple_of(index * count, 128), count), :]


def columns_at(ref, index, count):
    return ref[:, pl.ds(pl.multiple_of(index * count, 128), count)]


def send_x_kernel(ep_count, routes_ref, gates_ref, x_ref, out_ref, gated_ref):
    one, gated_ref[...] = slot_choice(routes_ref, gates_ref, ep_count)
    out_ref[...] = contract(one, x_ref[...], 1, 0).astype(jnp.bfloat16)


def send_y_kernel(gated_ref, dy_ref, out_ref):
    out_ref[...] = contract(gated_ref[...], dy_ref[...], 1, 0).astype(jnp.bfloat16)


def pre_kernel(ep_count, me_ref, routes_ref, x0, x1, x2, wg_ref, wu_ref, gate_ref, up_ref, choice_ref):
    width = x0.shape[1]
    for offset, x in zip(ORDER, (x0, x1, x2)):
        at = lax.rem(me_ref[0] + offset, 4)
        gate = contract(x[...], rows_at(wg_ref, at, width), 1, 0)
        up = contract(x[...], rows_at(wu_ref, at, width), 1, 0)
        if x is x0:
            gate_ref[...] = gate
            up_ref[...] = up
        else:
            gate_ref[...] += gate
            up_ref[...] += up
    choice_ref[...], _ = slot_choice(routes_ref, None, ep_count)


def back_kernel(me_ref, y0, y1, y2, wd_ref, back_ref):
    width = y0.shape[1]
    for offset, y in zip(ORDER, (y0, y1, y2)):
        at = lax.rem(me_ref[0] + offset, 4)
        back = contract(y[...], columns_at(wd_ref, at, width), 1, 1)
        if y is y0:
            back_ref[...] = back
        else:
            back_ref[...] += back


def mid_kernel(
    me_ref, x30, x31, y30, y31, gate_ref, up_ref, back_ref, wg_ref, wu_ref, wd_ref,
    dg_ref, du_ref, gh_ref, p0_ref, p1_ref,
):
    half = x30.shape[1]
    width = 2 * half
    far = lax.rem(me_ref[0] + 2, 4)
    wg = rows_at(wg_ref, far, width)
    wu = rows_at(wu_ref, far, width)
    wd = columns_at(wd_ref, far, width)
    gate_pre = gate_ref[...]
    up_pre = up_ref[...]
    d_hidden = back_ref[...]
    for h, (x, y) in enumerate(((x30, y30), (x31, y31))):
        span = slice(h * half, (h + 1) * half)
        gate_pre += contract(x[...], wg[span], 1, 0)
        up_pre += contract(x[...], wu[span], 1, 0)
        d_hidden += contract(y[...], wd[:, span], 1, 1)
    sigmoid = jax.nn.sigmoid(gate_pre)
    swish = gate_pre * sigmoid
    dg = (d_hidden * up_pre * sigmoid * (1.0 + gate_pre * (1.0 - sigmoid))).astype(jnp.bfloat16)
    du = (d_hidden * swish).astype(jnp.bfloat16)
    dg_ref[...] = dg
    du_ref[...] = du
    gh_ref[...] = (swish * up_pre).astype(jnp.bfloat16)
    for p_ref, rows in ((p0_ref, slice(0, SHIFTED)), (p1_ref, slice(SHIFTED, width))):
        p_ref[...] = (contract(dg, wg[rows], 1, 1) + contract(du, wu[rows], 1, 1)).astype(
            jnp.bfloat16
        )


def part_kernel(me_ref, dg_ref, du_ref, wg_ref, wu_ref, r0_ref, r1_ref, l0_ref, l1_ref, own_ref):
    width = own_ref.shape[1]
    for offset, outs in ((3, (l0_ref, l1_ref)), (1, (r0_ref, r1_ref)), (0, (own_ref,))):
        at = lax.rem(me_ref[0] + offset, 4)
        wg = rows_at(wg_ref, at, width)
        wu = rows_at(wu_ref, at, width)
        part = contract(dg_ref[...], wg, 1, 1) + contract(du_ref[...], wu, 1, 1)
        part = part.astype(jnp.bfloat16)
        if len(outs) == 1:
            own_ref[...] = part
        else:
            outs[0][...] = part[:, :SHIFTED]
            outs[1][...] = part[:, SHIFTED:]


def sum_kernel(own_ref, l_ref, r_ref, out_ref):
    total = own_ref[:, :SHIFTED].astype(jnp.float32)
    total = total + l_ref[...].astype(jnp.float32) + r_ref[...].astype(jnp.float32)
    out_ref[...] = total.astype(jnp.bfloat16)


def pack_kernel(section_ref, own_ref, l_ref, r_ref, shifted_ref, out_ref):
    rows = own_ref.shape[0]
    here = pl.multiple_of(section_ref[0] * rows, 128)
    there = pl.multiple_of((1 - section_ref[0]) * rows, 128)
    total = own_ref[:, SHIFTED:].astype(jnp.float32)
    total = total + l_ref[...].astype(jnp.float32) + r_ref[...].astype(jnp.float32)
    out_ref[pl.ds(there, rows), :] = total.astype(jnp.bfloat16)
    out_ref[pl.ds(here, rows), :SHIFTED] = shifted_ref[...]
    unused = out_ref.shape[1] - SHIFTED
    if unused:
        out_ref[pl.ds(here, rows), SHIFTED:] = jnp.zeros((rows, unused), jnp.bfloat16)


def grad_kernel(me_ref, *refs):
    x, y = refs[0:5], refs[5:10]
    dg, du, gh, out_g, out_u, out_d = refs[10:]
    step = pl.program_id(0)
    for d in range(4):

        @pl.when(step == d)
        def _(d=d):
            for n, (x_ref, y_ref) in enumerate(zip(x[d : d + 1 + d // 3], y[d : d + 1 + d // 3])):
                count = x_ref.shape[1]
                span = slice(n * count, (n + 1) * count)
                out_g[span, :] = contract(x_ref[...], dg[...], 0, 0).astype(jnp.bfloat16)
                out_u[span, :] = contract(x_ref[...], du[...], 0, 0).astype(jnp.bfloat16)
                out_d[:, span] = contract(gh[...], y_ref[...], 0, 0).astype(jnp.bfloat16)


def combine_kernel(section_ref, choice_ref, rows_ref, out_ref):
    slots = choice_ref.shape[0]
    shifted = rows_at(rows_ref, section_ref[0], slots)[:, :SHIFTED]
    out_ref[:, :SHIFTED] = contract(choice_ref[...], shifted, 0, 0).astype(jnp.bfloat16)
    rest = rows_at(rows_ref, 1 - section_ref[0], slots)
    out_ref[:, SHIFTED:] = contract(choice_ref[...], rest, 0, 0).astype(jnp.bfloat16)


def bf16(*shape):
    return jax.ShapeDtypeStruct(shape, jnp.bfloat16)


def f32(*shape):
    return jax.ShapeDtypeStruct(shape, jnp.float32)


IN_VMEM = pl.BlockSpec(memory_space=pltpu.VMEM)
IN_SMEM = pl.BlockSpec(memory_space=pltpu.SMEM)


def whole(array):
    return pl.BlockSpec(array.shape, lambda *_: (0,) * len(array.shape), pipeline_mode=pl.Buffered(1))


def in_hbm(array):
    return pltpu.with_memory_space_constraint(array, pltpu.HBM)


def call(kernel, outs, scalars, arrays, products=0):
    return pl.pallas_call(
        kernel,
        out_shape=outs,
        in_specs=[IN_SMEM] * len(scalars) + [IN_VMEM] * len(arrays),
        out_specs=[IN_VMEM] * len(outs),
        compiler_params=pltpu.CompilerParams(vmem_limit_bytes=16 * MIB),
        cost_estimate=pl.CostEstimate(flops=4 * products, bytes_accessed=0, transcendentals=0),
    )(*scalars, *arrays)


SHIFTED = 640
ORDER = (0, 3, 1, 2)


def slice_at(step, me_ref):
    offset = jnp.int32(ORDER[3])
    for d in range(3):
        offset = jnp.where(step == d, ORDER[d], offset)
    return lax.rem(me_ref[0] + offset, 4)


def body(tokens, out_grads, gates, routes, w_gate, w_up, w_down):
    ep_count = lax.axis_size("ep")
    token_count, width = tokens.shape[1:]
    rows = ep_count * CAP
    hidden = w_gate.shape[3]
    half = width // 2
    one_slice = rows * width * hidden
    w_gate, w_up, w_down = w_gate[0, 0], w_up[0, 0], w_down[0, 0]
    me = lax.axis_index("edp").astype(jnp.int32).reshape(1)
    section = lax.axis_index("section").astype(jnp.int32).reshape(1)

    routes, me, section = lax.optimization_barrier((routes[0].T, me, section))
    next_routes = passed_along(routes, "section", -1)

    send_x, gated = call(
        lambda *refs: send_x_kernel(ep_count, *refs),
        [bf16(rows, width), bf16(rows, token_count)],
        (),
        (routes, gates[0].T, tokens[0]),
        rows * token_count * (width + token_count),
    )
    (send_y,) = call(
        send_y_kernel, [bf16(rows, width)], (), (gated, out_grads[0]), rows * token_count * width
    )

    def to_experts(array):
        shaped = array.reshape(ep_count, CAP, width)
        return lax.all_to_all(shaped, "ep", split_axis=0, concat_axis=0, tiled=True).reshape(
            rows, width
        )

    own_x = to_experts(send_x)
    send_y, own_x = lax.optimization_barrier((send_y, own_x))
    x_left = passed_along(own_x, "edp", 1)
    x_right = passed_along(own_x, "edp", -1)
    own_y, x_left, x_right = lax.optimization_barrier((to_experts(send_y), x_left, x_right))
    x_far0 = passed_along(x_left[:, :half], "edp", 1)
    x_far1 = passed_along(x_right[:, half:], "edp", -1)
    y_right = passed_along(own_y, "edp", -1)
    y_left = passed_along(own_y, "edp", 1)

    gate_pre, up_pre, choice = call(
        lambda *refs: pre_kernel(ep_count, *refs),
        [f32(rows, hidden), f32(rows, hidden), bf16(rows, token_count)],
        (me,),
        (next_routes, own_x, x_left, x_right, w_gate, w_up),
        6 * one_slice,
    )
    y_left, y_right, gate_pre, up_pre, choice = lax.optimization_barrier(
        (y_left, y_right, gate_pre, up_pre, choice)
    )
    y_far0 = passed_along(y_left[:, :half], "edp", 1)
    y_far1 = passed_along(y_right[:, half:], "edp", -1)
    (back,) = call(
        back_kernel,
        [f32(rows, hidden)],
        (me,),
        (own_y, y_left, y_right, w_down),
        3 * one_slice,
    )
    parts = [bf16(rows, SHIFTED), bf16(rows, width - SHIFTED)]
    d_gate, d_up, gated_hidden, far0, far1 = call(
        mid_kernel,
        [bf16(rows, hidden)] * 3 + parts,
        (me,),
        (x_far0, x_far1, y_far0, y_far1, gate_pre, up_pre, back, w_gate, w_up, w_down),
        5 * one_slice,
    )
    far0 = passed_along(far0, "edp", 1)
    far1 = passed_along(far1, "edp", -1)
    right0, right1, left0, left1, own = call(
        part_kernel,
        parts * 2 + [bf16(rows, width)],
        (me,),
        (d_gate, d_up, w_gate, w_up),
        6 * one_slice,
    )

    def added(a, b):
        return (a.astype(jnp.float32) + b.astype(jnp.float32)).astype(jnp.bfloat16)

    from_right0 = passed_along(left0, "edp", -1)
    from_left0 = passed_along(added(right0, far0), "edp", 1)
    (shifted,) = call(sum_kernel, parts[:1], (), (own, from_left0, from_right0))
    shifted, right1, left1 = lax.optimization_barrier((shifted, right1, added(left1, far1)))
    from_left1 = passed_along(right1, "edp", 1)
    from_right1 = passed_along(left1, "edp", -1)
    shifted = passed_along(shifted, "section", -1)
    (packed,) = call(
        pack_kernel,
        [bf16(2 * rows, max(SHIFTED, width - SHIFTED))],
        (section,),
        (own, from_left1, from_right1, shifted),
    )
    packed, d_gate, d_up, gated_hidden = lax.optimization_barrier(
        (packed, d_gate, d_up, gated_hidden)
    )
    x = (own_x, x_left, x_right, x_far0, x_far1)
    y = (own_y, y_left, y_right, y_far0, y_far1)
    smalls = (d_gate, d_up, gated_hidden)
    grad_gate, grad_up, grad_down = pl.pallas_call(
        grad_kernel,
        out_shape=[bf16(4 * width, hidden)] * 2 + [bf16(hidden, 4 * width)],
        grid_spec=pltpu.PrefetchScalarGridSpec(
            num_scalar_prefetch=1,
            grid=(4,),
            in_specs=[whole(a) for a in (*x, *y, *smalls)],
            out_specs=[
                pl.BlockSpec((width, hidden), lambda i, m: (slice_at(i, m), 0)),
                pl.BlockSpec((width, hidden), lambda i, m: (slice_at(i, m), 0)),
                pl.BlockSpec((hidden, width), lambda i, m: (0, slice_at(i, m))),
            ],
        ),
        compiler_params=pltpu.CompilerParams(vmem_limit_bytes=28 * MIB),
        cost_estimate=pl.CostEstimate(
            flops=4 * 12 * one_slice, bytes_accessed=0, transcendentals=0
        ),
    )(me, *(in_hbm(a) for a in (*x, *y, *smalls)))
    returned = lax.all_to_all(
        packed.reshape(2 * ep_count, CAP, -1),
        ("section", "ep"),
        split_axis=0,
        concat_axis=0,
        tiled=True,
    ).reshape(2 * rows, -1)
    (grad_prev,) = call(
        combine_kernel,
        [bf16(token_count, width)],
        (section,),
        (choice, returned),
        rows * token_count * width,
    )
    return (grad_prev[None], grad_gate[None, None], grad_up[None, None], grad_down[None, None])


def solution(mesh):
    placed = (
        P("section", "ep", "edp"),
        P("section", "ep", "edp"),
        P("section", "ep", None),
        P("section", "ep", None),
        P("section", "ep", None, "edp"),
        P("section", "ep", None, "edp"),
        P("section", "ep", "edp", None),
    )
    return jax.shard_map(
        body,
        mesh=mesh,
        in_specs=placed,
        out_specs=(
            P("section", "ep", "edp"),
            P("section", "ep", None, "edp"),
            P("section", "ep", None, "edp"),
            P("section", "ep", "edp", None),
        ),
        check_vma=False,
    )
```
